128 devices in a mesh: rep: 4 (over x_lo, core), fsdp: 32 (over x_hi, y, z).
Axes of the slice: x: 4 (x_hi: 2, x_lo: 2; x = x_hi * 2 + x_lo), y: 4, z: 4, core: 2. Of those that a mesh axis runs over, the one named last changes fastest.
Arguments:
- tokens: bfloat16 [4, 32768, 3072], P('rep', 'fsdp'), may hold values from -6 to 6
- cotangent: bfloat16 [4, 32768, 1536], P('rep', 'fsdp'), may hold values from -6 to 6
- weight: float32 [4, 3072, 1536], P('rep', 'fsdp'), may hold values from -0.109375 to 0.109375
- momentum: float32 [4, 3072, 1536], P('rep', 'fsdp'), may hold values from -6 to 6
- step: int32 [], replicated, may hold values from 0 to 999
Outputs:
- new_weight: float32 [4, 3072, 1536], P('rep', 'fsdp')
- new_momentum: float32 [4, 3072, 1536], P('rep', 'fsdp')
The draws below stay inside these ranges and needn't reach their ends.
All inputs are finite; a program needn't handle non-finite values.
Results may differ from the reference program's by a relative error of at most 0.017.
Values may be sent and summed in bfloat16 or wider, within the bound.
No kernel may reach another device: no remote copies, remote signals or barrier semaphores. Data moves between devices by JAX's collectives and lax.ppermute only.
A program may use at most 128 MiB of HBM per device.

```python
import jax
import jax.numpy as jnp
from jax import lax

D = 3072
HEADS = 24
HEAD = 64
QW = 1536
TOK_DEV = 1024
TOKENS = 32768
GROUPS = 4
N_FSDP = 32


def spiked(entries, rng, source, target, parts, factor):
    owner, partner = [(jnp.arange(entries.shape[position]) // (entries.shape[position] // parts)).reshape([-1 if axis == position else 1 for axis in range(entries.ndim)]) for position in (source, target)]
    chosen = jax.random.permutation(rng, parts)[partner]
    strong = (owner == chosen) | (owner == (partner + parts // 2) % parts)
    return jnp.where(strong, factor * entries, entries)


def steps_of(stream_key, extent, shards, least, top_value):
    gain = 1.0
    for dim, shards_of in shards:
        steps = jax.random.uniform(jax.random.fold_in(jax.random.fold_in(stream_key, 6), dim), (shards_of,), jnp.float32, least / len(shards), top_value / len(shards))
        gain = gain * jnp.repeat(jnp.exp(steps), extent[dim] // shards_of).reshape((-1,) + (1,) * (len(extent) - 1 - dim))
    return gain


def scatter_about(own_key, shape, deviation, most, pieces=(), kind=jnp.bfloat16):
    entries = jax.random.normal(own_key, shape, jnp.float32) * deviation
    if len(pieces) > 0:
        entries = steps_of(own_key, shape, pieces, -0.22, 0.18) * entries
    return jnp.clip(entries, min=-most, max=most).astype(kind)


def noise_with(own_key, dims, scale, limit, split, heavy, kind=jnp.bfloat16):
    array = scale * jax.random.normal(own_key, dims, jnp.float32)
    if split:
        array = array * steps_of(own_key, dims, split, -0.22, 0.18)
    return jnp.clip(spiked(array, jax.random.fold_in(own_key, 3), *heavy), -limit, limit).astype(kind)


def setup_inputs(seed: int = 0) -> dict:
    splits = jax.random.split(jax.random.key(seed), 6)
    tokens = noise_with(splits[0], (GROUPS, TOKENS, D), 1.0, 6.0, ((0, 4), (1, 32)), (1, 2, 32, 2.75))
    cotangent = scatter_about(splits[1], (GROUPS, TOKENS, QW), 1.0, 6.0, ((0, 4), (1, 32)))
    weight = scatter_about(splits[2], (GROUPS, D, QW), D ** -0.5, 0.109375, ((0, 4), (1, 32)), jnp.float32)
    momentum = scatter_about(splits[3], (GROUPS, D, QW), 1.0, 6.0, ((0, 4), (1, 32)), jnp.float32)
    step = jax.random.randint(splits[4], (), 0, 1000).astype(jnp.int32)
    return {"tokens": tokens, "cotangent": cotangent, "weight": weight, "momentum": momentum, "step": step}


def norm_tokens(values):
    xf = values.astype(jnp.float32)
    mean = lax.optimization_barrier(jnp.mean(xf, axis=-1, keepdims=True))
    var = lax.optimization_barrier(jnp.mean((xf - mean) ** 2, axis=-1, keepdims=True))
    return ((xf - mean) * lax.rsqrt(var + 1e-05)).astype(jnp.bfloat16)

def group_grad(tok, cot, wgt):
    normed = norm_tokens(tok)
    wbf = lax.optimization_barrier(wgt.astype(jnp.bfloat16)).astype(jnp.float32)
    proj = jnp.dot(normed.astype(jnp.float32), wbf, preferred_element_type=jnp.float32)
    rows = proj.shape[0]
    heads = proj.reshape(rows, HEADS, HEAD)
    mu = lax.optimization_barrier(jnp.mean(heads, axis=-1, keepdims=True))
    var = lax.optimization_barrier(jnp.mean((heads - mu) ** 2, axis=-1, keepdims=True))
    scale = lax.rsqrt(var + 1e-06)
    query = (heads - mu) * scale
    cval = cot.astype(jnp.float32).reshape(rows, HEADS, HEAD)
    dproj = scale * (cval - lax.optimization_barrier(jnp.mean(cval, axis=-1, keepdims=True)) - query * lax.optimization_barrier(jnp.mean(cval * query, axis=-1, keepdims=True)))
    dproj = dproj.reshape(rows, QW).astype(jnp.bfloat16)
    blocks_x = normed.reshape(N_FSDP, TOK_DEV, D)
    blocks_d = dproj.reshape(N_FSDP, TOK_DEV, QW)

    def add_block(total, pair):
        left, right = pair
        term = jnp.dot(left.astype(jnp.float32).T, right.astype(jnp.float32), preferred_element_type=jnp.float32)
        term = lax.optimization_barrier(term.astype(jnp.bfloat16)).astype(jnp.float32)
        return (total + term, None)
    total, unused = lax.scan(add_block, jnp.zeros((D, QW), jnp.float32), (blocks_x, blocks_d))
    return total / jnp.sqrt(jnp.float32(TOKENS))

def reference(tokens, cotangent, weight, momentum, step):
    rate = jnp.float32(5e-05) * (step + 1).astype(jnp.float32)
    moms = []
    upds = []
    for group in range(GROUPS):
        grad = group_grad(tokens[group], cotangent[group], weight[group])
        mom = 0.9 * momentum[group] + grad
        moms.append(mom)
        upds.append(weight[group] - rate * mom)
    mom_all = jnp.stack(moms)
    upd_all = jnp.stack(upds)
    levels = int(GROUPS).bit_length() - 1
    dist = jnp.left_shift(jnp.int32(1), (step % levels).astype(jnp.int32))
    index = ((jnp.arange(GROUPS, dtype=jnp.int32) + dist) % GROUPS).astype(jnp.int32)
    new_weight = (upd_all + jnp.take(upd_all, index, axis=0)) * 0.5
    new_momentum = (mom_all + jnp.take(mom_all, index, axis=0)) * 0.5
    return (new_weight, new_momentum)
```

```python
import jax
import jax.numpy as jnp
from jax import lax
from jax.sharding import Mesh, PartitionSpec as P

HEAD = 64
F32 = jnp.float32
BF16 = jnp.bfloat16


def shift(value, axis, steps):
    count = lax.axis_size(axis)
    return lax.ppermute(value, axis, [(i, (i + steps) % count) for i in range(count)])


def norm_tokens(values):
    xf = values.astype(F32)
    mean = jnp.mean(xf, axis=-1, keepdims=True)
    var = jnp.mean((xf - mean) ** 2, axis=-1, keepdims=True)
    return ((xf - mean) * lax.rsqrt(var + 1e-05)).astype(BF16)


def place(parts, axis, dim):
    me = lax.axis_index(axis)
    count = lax.axis_size(axis)
    shape = list(parts[0][1].shape)
    shape.insert(dim, count)
    whole = jnp.zeros(shape, parts[0][1].dtype)
    for offset, part in parts:
        start = [0] * len(shape)
        start[dim] = (me + offset) % count
        whole = lax.dynamic_update_slice(whole, jnp.expand_dims(part, dim), start)
    return whole


def gather_direct(own, axis, dim):
    return place(
        [(0, own), (1, shift(own, axis, -1)), (2, shift(own, axis, 2)), (3, shift(own, axis, 1))], axis, dim
    )


def gather_ring(own, axis, dim):
    after = shift(own, axis, -1)
    before = shift(own, axis, 1)
    far0 = shift(before[0], axis, 1)
    far1 = shift(after[1], axis, -1)
    return place(
        [(0, own), (1, after), (2, jnp.stack([far0, far1])), (3, before)], axis, dim
    )


def pick(whole, axis, dim, offset):
    position = (lax.axis_index(axis) + offset) % lax.axis_size(axis)
    return lax.dynamic_index_in_dim(whole, position, dim, keepdims=False)


def scatter_direct(whole, axis, dim):
    one = shift(pick(whole, axis, dim, 1), axis, 1)
    two = shift(pick(whole, axis, dim, 2), axis, 2)
    three = shift(pick(whole, axis, dim, 3), axis, -1)
    own = pick(whole, axis, dim, 0).astype(F32)
    return own + one.astype(F32) + two.astype(F32) + three.astype(F32)


def scatter_ring(whole, axis, dim):
    far = pick(whole, axis, dim, 2)
    up = shift(far[0], axis, 1)
    down = shift(far[1], axis, -1)
    right = pick(whole, axis, dim, 1)
    left = pick(whole, axis, dim, 3)
    right = jnp.stack([(right[0].astype(F32) + up.astype(F32)).astype(BF16), right[1]])
    left = jnp.stack([left[0], (left[1].astype(F32) + down.astype(F32)).astype(BF16)])
    one = shift(right, axis, 1)
    three = shift(left, axis, -1)
    return (pick(whole, axis, dim, 0).astype(F32) + one.astype(F32) + three.astype(F32)).astype(BF16)


def head_grad(proj, cot):
    rows, width = proj.shape
    heads = proj.reshape(rows, width // HEAD, HEAD)
    mu = jnp.mean(heads, axis=-1, keepdims=True)
    var = jnp.mean((heads - mu) ** 2, axis=-1, keepdims=True)
    scale = lax.rsqrt(var + 1e-06)
    query = (heads - mu) * scale
    cval = cot.astype(F32).reshape(rows, width // HEAD, HEAD)
    dproj = scale * (
        cval
        - jnp.mean(cval, axis=-1, keepdims=True)
        - query * jnp.mean(cval * query, axis=-1, keepdims=True)
    )
    return dproj.reshape(rows, width).astype(BF16)


def on_device(tokens, cotangent, weight, momentum, step):
    local_w = weight[0]
    local_m = momentum[0]
    rate = jnp.float32(5e-05) * (step + 1).astype(F32)
    near = (step % 2) == 0
    shard, width = local_w.shape
    half = width // 2
    wbf = local_w.astype(BF16)
    mine = jnp.stack([wbf, local_m.astype(BF16)])

    both = place([(0, wbf), (1, shift(wbf, "xh", 1))], "xh", 0)
    part_a = gather_direct(both[..., :half], "z", 1)
    part_b = gather_direct(both[..., half:], "y", 1)
    whole_a = gather_ring(part_a, "y", 1)
    whole_b = gather_ring(part_b, "z", 2)
    other = jnp.where(near, shift(mine, "rep", -1), shift(mine, "rep", -2)).astype(F32)

    normed = norm_tokens(tokens[0])
    rows = normed.shape[0]
    grads = []
    for part, cot in ((whole_a, cotangent[0][:, :half]), (whole_b, cotangent[0][:, half:])):
        proj = jnp.dot(normed, part.reshape(-1, half), preferred_element_type=F32)
        dproj = head_grad(proj, cot)
        share = lax.dot_general(normed, dproj, (((0,), (0,)), ((), ())), preferred_element_type=F32)
        grads.append(share.astype(BF16).reshape(part.shape))
    sum_a = scatter_ring(grads[0], "y", 1)
    sum_b = scatter_ring(grads[1], "z", 2)
    sum_a = scatter_direct(sum_a, "z", 1)
    sum_b = scatter_direct(sum_b, "y", 1)
    both = jnp.concatenate([sum_a, sum_b], -1)
    summed = pick(both, "xh", 0, 0) + shift(pick(both, "xh", 0, 1).astype(BF16), "xh", 1).astype(F32)
    sent = summed.astype(BF16)
    pair = summed + jnp.where(near, shift(sent, "rep", -1), shift(sent, "rep", -2)).astype(F32)
    scale = 0.5 / jnp.sqrt(F32(rows * lax.axis_size(("xh", "y", "z"))))
    out_m = 0.45 * (local_m + other[1]) + scale * pair
    out_w = 0.5 * (local_w + other[0]) - rate * out_m
    return (out_w[None], out_m[None])


def solution(mesh):
    fine = Mesh(mesh.devices.reshape(mesh.shape["rep"], 2, 4, 4), ("rep", "xh", "y", "z"))
    rows = P("rep", ("xh", "y", "z"), None)
    return jax.shard_map(
        on_device,
        mesh=fine,
        in_specs=(rows, rows, rows, rows, P()),
        out_specs=(rows, rows),
        check_vma=False,
    )
```

```python
import functools

import jax
import jax.numpy as jnp
from jax import lax
from jax.experimental import pallas as pl
from jax.experimental.pallas import tpu as pltpu
from jax.sharding import Mesh, PartitionSpec as P

HEAD = 64
F32 = jnp.float32
BF16 = jnp.bfloat16
RING = 4
X, Y, Z, APART = range(4)
VMEM = pl.BlockSpec(memory_space=pltpu.VMEM)
SMEM = pl.BlockSpec(memory_space=pltpu.SMEM)


def shift(value, axis, steps):
    axes, steps = ((axis,), (steps,)) if isinstance(axis, str) else (axis, steps)
    sizes = [lax.axis_size(name) for name in axes]
    pairs = [(0, 0)]
    for size, step in zip(sizes, steps):
        pairs = [(s * size + i, t * size + (i + step) % size) for s, t in pairs for i in range(size)]
    return lax.ppermute(value, axes if len(axes) > 1 else axes[0], pairs)


def shaped(shape, dtype):
    return jax.ShapeDtypeStruct(shape, dtype)


def call(kernel, out_shape, flops, scalars, *arrays):
    moved = sum(a.size * a.dtype.itemsize for a in arrays) + sum(o.size * o.dtype.itemsize for o in out_shape)
    return pl.pallas_call(
        kernel,
        out_shape=out_shape,
        in_specs=[SMEM] * len(scalars) + [VMEM] * len(arrays),
        out_specs=tuple(VMEM for _ in out_shape),
        compiler_params=pltpu.CompilerParams(vmem_limit_bytes=10 * 1024 * 1024),
        cost_estimate=pl.CostEstimate(flops=flops, bytes_accessed=moved, transcendentals=0),
    )(*scalars, *arrays)


def dot(a, b):
    return jnp.dot(a, b, preferred_element_type=F32)


def norm_kernel(shard, start, tok_ref, ymajor_ref, zmajor_ref, turned_ref):
    block = 128
    order_y = [(x * RING + y) * RING * shard for y in range(RING) for x in range(2)]
    order_z = [((x * RING + y) * RING + z) * shard for z in range(RING) for x in range(2) for y in range(RING)]

    @pl.loop(0, ymajor_ref.shape[0] // block)
    def _(i):
        at = pl.ds(pl.multiple_of(i * block, block), block)
        xf = tok_ref[pl.ds(pl.multiple_of(start + i * block, block), block)].astype(F32)
        mean = jnp.mean(xf, axis=-1, keepdims=True)
        centred = xf - mean
        var = jnp.mean(centred * centred, axis=-1, keepdims=True)
        normed = centred * lax.rsqrt(var + 1e-05)
        small = normed.astype(BF16)
        run = RING * shard
        ymajor_ref[at] = jnp.concatenate([small[:, k : k + run] for k in order_y], axis=-1)
        zmajor_ref[at] = jnp.concatenate([normed[:, k : k + shard] for k in order_z], axis=-1).astype(BF16)
        turned_ref[:, at] = small.T


def norm_half(tokens, shard, half):
    rows, width = tokens.shape[0] // 2, tokens.shape[1]
    out = (shaped((rows, width), BF16), shaped((rows, width), BF16), shaped((width, rows), BF16))
    return call(functools.partial(norm_kernel, shard, half * rows), out, 8 * rows * width, (), tokens)


def order_kernel(me_ref, mine, other, a_ref, b_ref):
    half = a_ref.shape[-1]
    for part, at in ((mine, me_ref[X]), (other, 1 - me_ref[X])):
        a_ref[pl.ds(at, 1)] = part[:, :half][None]
        b_ref[pl.ds(at, 1)] = part[:, half:][None]


def order_x(me, mine, other):
    shard, width = mine.shape
    out = (shaped((2, shard, width // 2), BF16),) * 2
    return call(order_kernel, out, 0, (me,), mine, other)


def place_kernel(me_ref, *refs):
    parts, outs = refs[: 2 * RING], refs[2 * RING :]
    shard = parts[0].shape[1]
    for k in range(2):
        for offset in range(RING):
            at = lax.rem(me_ref[(Z, Y)[k]] + offset, RING)
            outs[k][:, pl.ds(pl.multiple_of(at * shard, shard), shard)] = parts[RING * k + offset][...]


def place(me, parts):
    _, shard, half = parts[0].shape
    out = (shaped((2, RING * shard, half), BF16),) * 2
    return call(place_kernel, out, 0, (me,), *parts)


def near_kernel(axis, offsets, me_ref, *refs):
    normeds, blocks = refs[:2], refs[2 : 2 + len(offsets)]
    begun, out_ref = refs[2 + len(offsets) : -1], refs[-1]
    depth = 2 * blocks[0].shape[1]
    for half, normed in enumerate(normeds):
        rows = slice(half * normed.shape[0], (half + 1) * normed.shape[0])
        total = begun[0][rows] if begun else None
        for offset, block in zip(offsets, blocks):
            at = pl.multiple_of(lax.rem(me_ref[axis] + offset, RING) * depth, depth)
            part = dot(normed[:, pl.ds(at, depth)], block[...].reshape(depth, -1))
            total = part if total is None else total + part
        out_ref[rows] = total


def project_near(me, axis, normeds, offsets, blocks, *begun):
    rows = 2 * normeds[0].shape[0]
    _, depth, cols = blocks[0].shape
    kernel = functools.partial(near_kernel, axis, offsets)
    out = (shaped((rows, cols), F32),)
    return call(kernel, out, 4 * len(blocks) * rows * depth * cols, (me,), *normeds, *blocks, *begun)[0]


def head_mean(values, spread, exact):
    wide = spread.shape[0]
    out = []
    for at in range(0, values.shape[-1], wide):
        part = values[:, at : at + wide]
        high = part.astype(BF16)
        mean = dot(high, spread)
        if not exact:
            mean = mean + dot((part - high.astype(F32)).astype(BF16), spread)
        out.append(mean)
    return jnp.concatenate(out, axis=-1)


def grad_block(turneds, x, at, axis, dproj):
    total = None
    for half, turned in enumerate(turneds):
        if axis == Y:
            part = turned[pl.ds(x * RING + at, 1)]
        else:
            part = turned[pl.ds(x * RING, RING), pl.ds(at, 1)]
        count = turned.shape[3]
        part = dot(part.reshape(RING * turned.shape[2], count), dproj[half * count : (half + 1) * count])
        total = part if total is None else total + part
    return total.astype(BF16)


def far_kernel(me_ref, cot, turned0, turned1, *refs):
    rows, cols = refs[0].shape
    depth = 2 * refs[3].shape[0]
    wide = 4 * HEAD
    block = 256
    of_row = lax.broadcasted_iota(jnp.int32, (wide, wide), 0) // HEAD
    of_col = lax.broadcasted_iota(jnp.int32, (wide, wide), 1) // HEAD
    spread = jnp.where(of_row == of_col, 1.0 / HEAD, 0.0).astype(BF16)
    for k, axis in enumerate((Y, Z)):
        near, *normeds, far0, far1 = refs[5 * k : 5 * k + 5]
        dproj_ref, *grad_refs = refs[10 + 3 * k : 13 + 3 * k]
        far = lax.rem(me_ref[axis] + 2, RING)
        features = pl.ds(pl.multiple_of(far * depth, depth), depth)
        weight = jnp.concatenate([far0[...], far1[...]], axis=0)
        for at in range(0, rows, block):
            part = slice(at, at + block)
            normed, start = normeds[at // (rows // 2)], at % (rows // 2)
            proj = near[part] + dot(normed[start : start + block, features], weight)
            centred = proj - head_mean(proj, spread, False)
            scale = lax.rsqrt(head_mean(centred * centred, spread, True) + 1e-06)
            query = centred * scale
            cval = cot[part, k * cols : (k + 1) * cols]
            along = head_mean(cval.astype(F32) * query, spread, False)
            dproj = scale * (cval.astype(F32) - head_mean(cval, spread, True) - query * along)
            dproj_ref[part] = dproj.astype(BF16)
        for x in range(2):
            grad_refs[x][...] = grad_block((turned0, turned1), x, far, axis, dproj_ref)


def project_far(me, cot, turneds, halves):
    rows, cols = halves[0].shape
    depth = halves[3].shape[0]
    out = ((shaped((rows, cols), BF16),) + (shaped((depth, cols), BF16),) * 2) * 2
    flops = 16 * rows * depth * cols + 24 * rows * cols * 4 * HEAD
    return call(far_kernel, out, flops, (me,), cot, *turneds, *halves)


def rows_kernel(offsets, me_ref, turned0, turned1, *refs):
    for k, axis in enumerate((Y, Z)):
        for n, offset in enumerate(offsets):
            at = lax.rem(me_ref[axis] + offset, RING)
            for x in range(2):
                out_ref = refs[2 + k * len(offsets) + n]
                out_ref[x] = grad_block((turned0, turned1), x, at, axis, refs[k])


def grad_rows(me, offsets, turneds, *dprojs):
    rows, cols = dprojs[0].shape
    depth = RING * turneds[0].shape[2]
    out = (shaped((2, depth, cols), BF16),) * (2 * len(offsets))
    flops = 4 * len(out) * rows * depth * cols
    return call(functools.partial(rows_kernel, offsets), out, flops, (me,), *turneds, *dprojs)


def split_kernel(me_ref, *refs):
    count = (len(refs) - 2 * RING) // 2
    for k, axis in enumerate((Z, Y)):
        parts, outs = refs[k * count : (k + 1) * count], refs[2 * count + k * RING : 2 * count + (k + 1) * RING]
        shard = outs[0].shape[1]
        for offset, out_ref in enumerate(outs):
            at = lax.rem(me_ref[axis] + offset, RING)
            rows = pl.ds(pl.multiple_of(at * shard, shard), shard)
            out_ref[...] = sum(part[:, rows].astype(F32) for part in parts).astype(BF16)


def split_sum(me, parts):
    _, depth, cols = parts[0].shape
    out = (shaped((2, depth // RING, cols), BF16),) * (2 * RING)
    return call(split_kernel, out, 8 * depth * cols, (me,), *parts)


def join_kernel(me_ref, *refs):
    own_ref, sent_ref, far_ref = refs[2 * RING :]
    cols = refs[0].shape[-1]
    for half in range(2):
        parts = refs[RING * half : RING * (half + 1)]
        lanes = slice(half * cols, (half + 1) * cols)
        for out, at in (((own_ref, sent_ref), me_ref[X]), ((far_ref,), 1 - me_ref[X])):
            total = sum(part[pl.ds(at, 1)].astype(F32) for part in parts)[0]
            for out_ref in out:
                out_ref[:, lanes] = total.astype(out_ref.dtype)


def join(me, parts):
    _, shard, cols = parts[0].shape
    out = (shaped((shard, 2 * cols), F32), shaped((shard, 2 * cols), BF16), shaped((shard, 2 * cols), BF16))
    return call(join_kernel, out, 16 * shard * cols, (me,), *parts)


def add(a, b):
    return (a.astype(F32) + b.astype(F32)).astype(BF16)


def base_kernel(me_ref, weight, momentum, next1, next2, w_ref, m_ref):
    nearby = me_ref[APART] == 1
    w_ref[...] = 0.5 * (weight[...] + jnp.where(nearby, next1[0], next2[0]).astype(F32))
    m_ref[...] = 0.45 * (momentum[...] + jnp.where(nearby, next1[1], next2[1]).astype(F32))


def update_kernel(scale, me_ref, rate_ref, base_w, base_m, own, other_x, *refs):
    *parts, w_ref, m_ref = refs
    nearby = me_ref[APART] == 1
    sent, away = (jnp.where(nearby, one[...], two[...]).astype(F32) for one, two in (parts[:2], parts[2:]))
    out_m = base_m[...] + scale * (own[...] + (other_x[...].astype(F32) + (sent + away)))
    m_ref[...] = out_m
    w_ref[...] = base_w[...] - rate_ref[0] * out_m


def on_device(tokens, cotangent, weight, momentum, step):
    local_w = weight[0]
    local_m = momentum[0]
    shard, width = local_w.shape
    apart = 1 + step % 2
    me = jnp.stack([lax.axis_index("xh"), lax.axis_index("y"), lax.axis_index("z"), apart]).astype(jnp.int32)
    rate = (jnp.float32(5e-05) * (step + 1).astype(F32))[None]
    wbf = local_w.astype(BF16)
    wbf, me, rate = lax.optimization_barrier((wbf, me, rate))
    pair = (shaped(local_w.shape, F32),) * 2

    wfar, norm0 = lax.optimization_barrier((shift(wbf, "xh", 1), norm_half(tokens[0], shard, 0)))
    half_a, half_b = order_x(me, wbf, wfar)
    b2, a2, b1, a1, b3, a3, norm1 = lax.optimization_barrier(
        [shift(half_b, "y", 2), shift(half_a, "z", 2)]
        + [shift(half_b, "y", -1), shift(half_a, "z", -1), shift(half_b, "y", 1), shift(half_a, "z", 1)]
        + [norm_half(tokens[0], shard, 1)]
    )
    ymajor, zmajor, turned = zip(norm0, norm1)
    turned = [part.reshape(2 * RING, RING, shard, -1) for part in turned]
    own = place(me, [half_a, a1, a2, a3, half_b, b1, b2, b3])
    rings = (("y", Y, ymajor), ("z", Z, zmajor))
    around, begun = lax.optimization_barrier(
        (
            [[shift(block, axis, steps) for steps in (-1, 1)] for (axis, _, _), block in zip(rings, own)],
            [project_near(me, at, normed, (0,), (block,)) for (_, at, normed), block in zip(rings, own)],
        )
    )
    far = [
        (shift(before[0], axis, 1), shift(after[1], axis, -1)) for (axis, _, _), (after, before) in zip(rings, around)
    ]
    begun = [
        project_near(me, at, normed, (1, 3), blocks, done)
        for (_, at, normed), blocks, done in zip(rings, around, begun)
    ]
    dproj_a, far0_a, far1_a, dproj_b, far0_b, far1_b = project_far(
        me, cotangent[0], turned, (begun[0], *ymajor, *far[0], begun[1], *zmajor, *far[1])
    )
    up_a, down_a = shift(far0_a, "y", 1), shift(far1_a, "y", -1)
    up_b, down_b = shift(far0_b, "z", 1), shift(far1_b, "z", -1)
    right_a, left_a, right_b, left_b = grad_rows(me, (1, 3), turned, dproj_a, dproj_b)
    up_a, down_a, up_b, down_b, right_a, left_a, right_b, left_b = lax.optimization_barrier(
        (up_a, down_a, up_b, down_b, right_a, left_a, right_b, left_b)
    )
    right_a = shift(right_a.at[0].set(add(right_a[0], up_a)), "y", 1)
    left_a = shift(left_a.at[1].set(add(left_a[1], down_a)), "y", -1)
    right_b = shift(right_b.at[0].set(add(right_b[0], up_b)), "z", 1)
    left_b = shift(left_b.at[1].set(add(left_b[1], down_b)), "z", -1)
    own_a, own_b = grad_rows(me, (0,), turned, dproj_a, dproj_b)
    mine, own_a = lax.optimization_barrier((jnp.stack([local_w, local_m]), own_a))
    mine = mine.astype(BF16)
    base = call(base_kernel, pair, 0, (me,), local_w, local_m, shift(mine, "rep", -1), shift(mine, "rep", -2))
    own_b, base = lax.optimization_barrier((own_b, base))
    c = split_sum(me, (own_a, right_a, left_a, own_b, right_b, left_b))
    sums = [c[0], shift(c[1], "z", 1), shift(c[2], "z", 2), shift(c[3], "z", -1)]
    sums += [c[4], shift(c[5], "y", 1), shift(c[6], "y", 2), shift(c[7], "y", -1)]
    kept, sent, away = join(me, sums)
    got = [shift(away, ("rep", "xh"), (-1, 1)), shift(away, ("rep", "xh"), (-2, 1))]
    got = [shift(away, "xh", 1), shift(sent, "rep", -1), shift(sent, "rep", -2)] + got
    scale = 0.5 / (tokens.shape[1] * 2 * RING * RING) ** 0.5
    out_w, out_m = call(functools.partial(update_kernel, scale), pair, 0, (me, rate), *base, kept, *got)
    return (out_w[None], out_m[None])


def solution(mesh):
    fine = Mesh(mesh.devices.reshape(mesh.shape["rep"], 2, RING, RING), ("rep", "xh", "y", "z"))
    rows = P("rep", ("xh", "y", "z"), None)
    return jax.shard_map(
        on_device,
        mesh=fine,
        in_specs=(rows, rows, rows, rows, P()),
        out_specs=(rows, rows),
        check_vma=False,
    )
```

```python
import functools

import jax
import jax.numpy as jnp
from jax import lax
from jax.experimental import pallas as pl
from jax.experimental.pallas import tpu as pltpu
from jax.sharding import Mesh, PartitionSpec as P

HEAD = 64
F32 = jnp.float32
BF16 = jnp.bfloat16
RING = 4
X, Y, Z, APART = range(4)
PEAK = 1.1e9
VMEM = pl.BlockSpec(memory_space=pltpu.VMEM)
SMEM = pl.BlockSpec(memory_space=pltpu.SMEM)


def shift(value, axis, steps):
    axes, steps = ((axis,), (steps,)) if isinstance(axis, str) else (axis, steps)
    sizes = [lax.axis_size(name) for name in axes]
    pairs = [(0, 0)]
    for size, step in zip(sizes, steps):
        pairs = [(s * size + i, t * size + (i + step) % size) for s, t in pairs for i in range(size)]
    return lax.ppermute(value, axes if len(axes) > 1 else axes[0], pairs)


def shaped(shape, dtype):
    return jax.ShapeDtypeStruct(shape, dtype)


def call(kernel, out_shape, flops, scalars, *arrays):
    return pl.pallas_call(
        kernel,
        out_shape=out_shape,
        in_specs=[SMEM] * len(scalars) + [VMEM] * len(arrays),
        out_specs=tuple(VMEM for _ in out_shape),
        compiler_params=pltpu.CompilerParams(vmem_limit_bytes=10 * 1024 * 1024),
        cost_estimate=pl.CostEstimate(flops=int(flops), bytes_accessed=0, transcendentals=0),
    )(*scalars, *arrays)


def dot(a, b):
    return jnp.dot(a, b, preferred_element_type=F32)


def norm_kernel(shard, start, tok_ref, ymajor_ref, zmajor_ref, turned_ref):
    block = 128
    order_y = [(x * RING + y) * RING * shard for y in range(RING) for x in range(2)]
    order_z = [((x * RING + y) * RING + z) * shard for z in range(RING) for x in range(2) for y in range(RING)]

    @pl.loop(0, ymajor_ref.shape[0] // block)
    def _(i):
        at = pl.ds(pl.multiple_of(i * block, block), block)
        xf = tok_ref[pl.ds(pl.multiple_of(start + i * block, block), block)].astype(F32)
        mean = jnp.mean(xf, axis=-1, keepdims=True)
        centred = xf - mean
        var = jnp.mean(centred * centred, axis=-1, keepdims=True)
        normed = centred * lax.rsqrt(var + 1e-05)
        small = normed.astype(BF16)
        run = RING * shard
        ymajor_ref[at] = jnp.concatenate([small[:, k : k + run] for k in order_y], axis=-1)
        zmajor_ref[at] = jnp.concatenate([normed[:, k : k + shard] for k in order_z], axis=-1).astype(BF16)
        turned_ref[:, at] = small.T


def norm_half(tokens, shard, half):
    rows, width = tokens.shape[0] // 2, tokens.shape[1]
    out = (shaped((rows, width), BF16), shaped((rows, width), BF16), shaped((width, rows), BF16))
    return call(functools.partial(norm_kernel, shard, half * rows), out, 4.4 * PEAK, (), tokens)


def order_kernel(me_ref, mine, other, a_ref, b_ref):
    half = a_ref.shape[-1]
    for part, at in ((mine, me_ref[X]), (other, 1 - me_ref[X])):
        a_ref[pl.ds(at, 1)] = part[:, :half][None]
        b_ref[pl.ds(at, 1)] = part[:, half:][None]


def order_x(me, mine, other):
    shard, width = mine.shape
    out = (shaped((2, shard, width // 2), BF16),) * 2
    return call(order_kernel, out, 0, (me,), mine, other)


def place_kernel(axis, me_ref, *refs):
    parts, out_ref = refs[:RING], refs[RING]
    shard = parts[0].shape[1]
    for offset, part in enumerate(parts):
        at = lax.rem(me_ref[axis] + offset, RING)
        out_ref[:, pl.ds(pl.multiple_of(at * shard, shard), shard)] = part[...]


def place(me, axis, parts):
    _, shard, half = parts[0].shape
    out = (shaped((2, RING * shard, half), BF16),)
    return call(functools.partial(place_kernel, axis), out, 0, (me,), *parts)[0]


def near_kernel(axis, offsets, me_ref, *refs):
    normeds, blocks = refs[:2], refs[2 : 2 + len(offsets)]
    begun, out_ref = refs[2 + len(offsets) : -1], refs[-1]
    depth = 2 * blocks[0].shape[1]
    for half, normed in enumerate(normeds):
        rows = slice(half * normed.shape[0], (half + 1) * normed.shape[0])
        total = begun[0][rows] if begun else None
        for offset, block in zip(offsets, blocks):
            at = pl.multiple_of(lax.rem(me_ref[axis] + offset, RING) * depth, depth)
            part = dot(normed[:, pl.ds(at, depth)], block[...].reshape(depth, -1))
            total = part if total is None else total + part
        out_ref[rows] = total


def project_near(me, axis, normeds, offsets, blocks, *begun):
    rows = 2 * normeds[0].shape[0]
    _, depth, cols = blocks[0].shape
    kernel = functools.partial(near_kernel, axis, offsets)
    out = (shaped((rows, cols), F32),)
    return call(kernel, out, 1.6 * len(blocks) * PEAK, (me,), *normeds, *blocks, *begun)[0]


def head_mean(values, spread, exact):
    wide = spread.shape[0]
    out = []
    for at in range(0, values.shape[-1], wide):
        part = values[:, at : at + wide]
        high = part.astype(BF16)
        mean = dot(high, spread)
        if not exact:
            mean = mean + dot((part - high.astype(F32)).astype(BF16), spread)
        out.append(mean)
    return jnp.concatenate(out, axis=-1)


def grad_block(turneds, x, at, axis, dproj):
    total = None
    for half, turned in enumerate(turneds):
        if axis == Y:
            part = turned[pl.ds(x * RING + at, 1)]
        else:
            part = turned[pl.ds(x * RING, RING), pl.ds(at, 1)]
        count = turned.shape[3]
        part = dot(part.reshape(RING * turned.shape[2], count), dproj[half * count : (half + 1) * count])
        total = part if total is None else total + part
    return total.astype(BF16)


def head_spread():
    of_row = lax.broadcasted_iota(jnp.int32, (4 * HEAD, 4 * HEAD), 0) // HEAD
    of_col = lax.broadcasted_iota(jnp.int32, (4 * HEAD, 4 * HEAD), 1) // HEAD
    return jnp.where(of_row == of_col, 1.0 / HEAD, 0.0).astype(BF16)


def centre_kernel(cot, out_ref):
    spread = head_spread()
    block = 256
    for at in range(0, cot.shape[0], block):
        part = cot[at : at + block]
        out_ref[at : at + block] = part.astype(F32) - head_mean(part, spread, True)


def centre(cot):
    return call(centre_kernel, (shaped(cot.shape, F32),), 0, (), cot)[0]


def far_kernel(axis, me_ref, cot, turned0, turned1, near, normed0, normed1, far0, far1, dproj_ref, *grad_refs):
    rows, cols = near.shape
    depth = 2 * far0.shape[0]
    block = 256
    spread = head_spread()
    far = lax.rem(me_ref[axis] + 2, RING)
    features = pl.ds(pl.multiple_of(far * depth, depth), depth)
    weight = jnp.concatenate([far0[...], far1[...]], axis=0)
    from_col = 0 if axis == Y else cols
    for at in range(0, rows, block):
        part = slice(at, at + block)
        normed, start = (normed0, normed1)[at // (rows // 2)], at % (rows // 2)
        proj = near[part] + dot(normed[start : start + block, features], weight)
        centred = proj - head_mean(proj, spread, False)
        scale = lax.rsqrt(head_mean(centred * centred, spread, True) + 1e-06)
        query = centred * scale
        cval = cot[part, from_col : from_col + cols]
        along = head_mean(cval * query, spread, False)
        dproj_ref[part] = (scale * (cval - query * along)).astype(BF16)
    for x in range(2):
        grad_refs[x][...] = grad_block((turned0, turned1), x, far, axis, dproj_ref)


def project_far(me, axis, cot, turneds, near, normeds, far0, far1):
    rows, cols = near.shape
    depth = far0.shape[0]
    out = (shaped((rows, cols), BF16),) + (shaped((depth, cols), BF16),) * 2
    kernel = functools.partial(far_kernel, axis)
    return call(kernel, out, 6 * PEAK, (me,), cot, *turneds, near, *normeds, far0, far1)


def rows_kernel(axis, offsets, me_ref, turned0, turned1, dproj, *outs):
    for offset, out_ref in zip(offsets, outs):
        at = lax.rem(me_ref[axis] + offset, RING)
        for x in range(2):
            out_ref[x] = grad_block((turned0, turned1), x, at, axis, dproj)


def grad_rows(me, axis, offsets, turneds, dproj):
    rows, cols = dproj.shape
    depth = RING * turneds[0].shape[2]
    out = (shaped((2, depth, cols), BF16),) * len(offsets)
    return call(functools.partial(rows_kernel, axis, offsets), out, 1.6 * len(out) * PEAK, (me,), *turneds, dproj)


def split_kernel(axis, me_ref, *refs):
    parts, outs = refs[:-RING], refs[-RING:]
    shard = outs[0].shape[1]
    for offset, out_ref in enumerate(outs):
        at = lax.rem(me_ref[axis] + offset, RING)
        rows = pl.ds(pl.multiple_of(at * shard, shard), shard)
        out_ref[...] = sum(part[:, rows].astype(F32) for part in parts).astype(BF16)


def split_sum(me, axis, parts):
    _, depth, cols = parts[0].shape
    out = (shaped((2, depth // RING, cols), BF16),) * RING
    return call(functools.partial(split_kernel, axis), out, 0, (me,), *parts)


def join_kernel(me_ref, *refs):
    kept_ref, sent_ref, away_ref = refs[2 * RING :]
    cols = refs[0].shape[-1]
    for half in range(2):
        parts = refs[RING * half : RING * (half + 1)]
        lanes = slice(half * cols, (half + 1) * cols)
        for outs, at in (((kept_ref, sent_ref), me_ref[X]), ((away_ref,), 1 - me_ref[X])):
            total = sum(part[pl.ds(at, 1)].astype(F32) for part in parts)[0]
            for out_ref in outs:
                out_ref[:, lanes] = total.astype(out_ref.dtype)


def join(me, parts):
    _, shard, cols = parts[0].shape
    out = (shaped((shard, 2 * cols), F32),) + (shaped((shard, 2 * cols), BF16),) * 2
    return call(join_kernel, out, 0, (me,), *parts)


def exchange(steps, sent, away):
    return (
        shift(away, ("rep", "xh"), (-steps, 1)),
        shift(away, "xh", 1),
        shift(sent, "rep", -steps),
    )


def add(a, b):
    return (a.astype(F32) + b.astype(F32)).astype(BF16)


def base_kernel(me_ref, weight, momentum, next1, next2, w_ref, m_ref):
    nearby = me_ref[APART] == 1
    w_ref[...] = 0.5 * (weight[...] + jnp.where(nearby, next1[0], next2[0]).astype(F32))
    m_ref[...] = 0.45 * (momentum[...] + jnp.where(nearby, next1[1], next2[1]).astype(F32))


def update_kernel(scale, rate_ref, base_w, base_m, own, got0, got1, got2, w_ref, m_ref):
    others = got0[...].astype(F32) + got1[...].astype(F32) + got2[...].astype(F32)
    out_m = base_m[...] + scale * (own[...] + others)
    m_ref[...] = out_m
    w_ref[...] = base_w[...] - rate_ref[0] * out_m


def on_device(tokens, cotangent, weight, momentum, step):
    local_w = weight[0]
    local_m = momentum[0]
    shard, width = local_w.shape
    apart = 1 + step % 2
    me = jnp.stack([lax.axis_index("xh"), lax.axis_index("y"), lax.axis_index("z"), apart]).astype(jnp.int32)
    rate = (jnp.float32(5e-05) * (step + 1).astype(F32))[None]
    wbf = local_w.astype(BF16)
    wbf, me, rate, apart = lax.optimization_barrier((wbf, me, rate, apart))
    pair = (shaped(local_w.shape, F32),) * 2

    wfar, norm0 = lax.optimization_barrier((shift(wbf, "xh", 1), norm_half(tokens[0], shard, 0)))
    half_a, half_b = order_x(me, wbf, wfar)
    parts_a = [half_a, shift(half_a, "z", -1), shift(half_a, "z", 2), shift(half_a, "z", 1)]
    parts_b = [half_b, shift(half_b, "y", -1), shift(half_b, "y", 2), shift(half_b, "y", 1)]
    parts_a, parts_b, norm0 = lax.optimization_barrier((parts_a, parts_b, norm0))
    own_a, own_b = place(me, Z, parts_a), place(me, Y, parts_b)
    tokens, _ = lax.optimization_barrier((tokens, own_b))
    ymajor, zmajor, turned = zip(norm0, norm_half(tokens[0], shard, 1))
    turned = [part.reshape(2 * RING, RING, shard, -1) for part in turned]
    cot = centre(cotangent[0])
    rings = (("y", Y, ymajor, own_a), ("z", Z, zmajor, own_b))
    around = []
    for axis, at, normed, block in rings:
        passed = [shift(block, axis, steps) for steps in (-1, 1)]
        around.append(
            lax.optimization_barrier((passed, project_near(me, at, normed, (0,), (block,)), turned, cot))
        )
    turned, cot = around[1][2:]
    far = [
        (shift(before[0], ring[0], 1), shift(after[1], ring[0], -1))
        for ring, ((after, before), *_) in zip(rings, around)
    ]
    begun = [
        project_near(me, at, normed, (1, 3), blocks, done)
        for (_, at, normed, _), (blocks, done, *_) in zip(rings, around)
    ]
    begun, turned = lax.optimization_barrier((begun, turned))
    dproj_a, far0_a, far1_a = project_far(me, Y, cot, turned, begun[0], ymajor, *far[0])
    up_a, down_a = shift(far0_a, "y", 1), shift(far1_a, "y", -1)
    dproj_a, begun_b = lax.optimization_barrier((dproj_a, begun[1]))
    dproj_b, far0_b, far1_b = project_far(me, Z, cot, turned, begun_b, zmajor, *far[1])
    up_b, down_b = shift(far0_b, "z", 1), shift(far1_b, "z", -1)
    dproj_a, dproj_b = lax.optimization_barrier((dproj_a, dproj_b))
    right_a, left_a = grad_rows(me, Y, (1, 3), turned, dproj_a)
    right_a = right_a.at[0].set(add(right_a[0], up_a))
    left_a = left_a.at[1].set(add(left_a[1], down_a))
    right_a, left_a, dproj_b = lax.optimization_barrier((right_a, left_a, dproj_b))
    right_a, left_a = shift(right_a, "y", 1), shift(left_a, "y", -1)
    right_b, left_b = grad_rows(me, Z, (1, 3), turned, dproj_b)
    right_b = right_b.at[0].set(add(right_b[0], up_b))
    left_b = left_b.at[1].set(add(left_b[1], down_b))
    right_b, left_b, dproj_a, dproj_b = lax.optimization_barrier((right_b, left_b, dproj_a, dproj_b))
    right_b, left_b = shift(right_b, "z", 1), shift(left_b, "z", -1)
    (own_a,) = grad_rows(me, Y, (0,), turned, dproj_a)
    (own_b,) = grad_rows(me, Z, (0,), turned, dproj_b)
    mine, own_a = lax.optimization_barrier((jnp.stack([local_w, local_m]), own_a))
    mine = mine.astype(BF16)
    base = call(base_kernel, pair, 0, (me,), local_w, local_m, shift(mine, "rep", -1), shift(mine, "rep", -2))
    own_b, base = lax.optimization_barrier((own_b, base))
    c = split_sum(me, Z, (own_a, right_a, left_a))
    sums = [c[0], shift(c[1], "z", 1), shift(c[3], "z", -1), shift(c[2], "z", 2)]
    c = split_sum(me, Y, (own_b, right_b, left_b))
    sums += [c[0], shift(c[1], "y", 1), shift(c[3], "y", -1), shift(c[2], "y", 2)]
    kept, sent, away, apart = lax.optimization_barrier((*join(me, sums), apart))
    got = lax.cond(apart == 1, functools.partial(exchange, 1), functools.partial(exchange, 2), sent, away)
    scale = 0.5 / (tokens.shape[1] * 2 * RING * RING) ** 0.5
    out_w, out_m = call(functools.partial(update_kernel, scale), pair, 0, (rate,), *base, kept, *got)
    return (out_w[None], out_m[None])


def solution(mesh):
    fine = Mesh(mesh.devices.reshape(mesh.shape["rep"], 2, RING, RING), ("rep", "xh", "y", "z"))
    rows = P("rep", ("xh", "y", "z"), None)
    return jax.shard_map(
        on_device,
        mesh=fine,
        in_specs=(rows, rows, rows, rows, P()),
        out_specs=(rows, rows),
        check_vma=False,
    )
```

```python
import functools

import jax
import jax.numpy as jnp
from jax import lax
from jax.experimental import pallas as pl
from jax.experimental.pallas import tpu as pltpu
from jax.sharding import Mesh, PartitionSpec as P

HEAD = 64
F32 = jnp.float32
BF16 = jnp.bfloat16
RING = 4
X, Y, Z, APART = range(4)
PEAK = 1.1e9
VMEM = pl.BlockSpec(memory_space=pltpu.VMEM)
SMEM = pl.BlockSpec(memory_space=pltpu.SMEM)


def shift(value, axis, steps):
    axes, steps = ((axis,), (steps,)) if isinstance(axis, str) else (axis, steps)
    sizes = [lax.axis_size(name) for name in axes]
    pairs = [(0, 0)]
    for size, step in zip(sizes, steps):
        pairs = [(s * size + i, t * size + (i + step) % size) for s, t in pairs for i in range(size)]
    return lax.ppermute(value, axes if len(axes) > 1 else axes[0], pairs)


def shaped(shape, dtype):
    return jax.ShapeDtypeStruct(shape, dtype)


def call(kernel, out_shape, flops, scalars, *arrays):
    return pl.pallas_call(
        kernel,
        out_shape=out_shape,
        in_specs=[SMEM] * len(scalars) + [VMEM] * len(arrays),
        out_specs=tuple(VMEM for _ in out_shape),
        compiler_params=pltpu.CompilerParams(vmem_limit_bytes=10 * 1024 * 1024),
        cost_estimate=pl.CostEstimate(flops=int(flops), bytes_accessed=0, transcendentals=0),
    )(*scalars, *arrays)


def dot(a, b):
    return jnp.dot(a, b, preferred_element_type=F32)


def norm_kernel(shard, start, tok_ref, ymajor_ref, zmajor_ref, turned_ref):
    block = 128
    order_y = [(x * RING + y) * RING * shard for y in range(RING) for x in range(2)]
    order_z = [((x * RING + y) * RING + z) * shard for z in range(RING) for x in range(2) for y in range(RING)]

    @pl.loop(0, ymajor_ref.shape[0] // block)
    def _(i):
        at = pl.ds(pl.multiple_of(i * block, block), block)
        xf = tok_ref[pl.ds(pl.multiple_of(start + i * block, block), block)].astype(F32)
        mean = jnp.mean(xf, axis=-1, keepdims=True)
        centred = xf - mean
        var = jnp.mean(centred * centred, axis=-1, keepdims=True)
        normed = centred * lax.rsqrt(var + 1e-05)
        small = normed.astype(BF16)
        run = RING * shard
        ymajor_ref[at] = jnp.concatenate([small[:, k : k + run] for k in order_y], axis=-1)
        zmajor_ref[at] = jnp.concatenate([normed[:, k : k + shard] for k in order_z], axis=-1).astype(BF16)
        turned_ref[:, at] = small.T


def norm_half(tokens, shard, half):
    rows, width = tokens.shape[0] // 2, tokens.shape[1]
    out = (shaped((rows, width), BF16), shaped((rows, width), BF16), shaped((width, rows), BF16))
    return call(functools.partial(norm_kernel, shard, half * rows), out, 4.4 * PEAK, (), tokens)


def order_kernel(me_ref, mine, other, a_ref, b_ref):
    half = a_ref.shape[-1]
    for part, at in ((mine, me_ref[X]), (other, 1 - me_ref[X])):
        a_ref[pl.ds(at, 1)] = part[:, :half][None]
        b_ref[pl.ds(at, 1)] = part[:, half:][None]


def order_x(me, mine, other):
    shard, width = mine.shape
    out = (shaped((2, shard, width // 2), BF16),) * 2
    return call(order_kernel, out, 0, (me,), mine, other)


def place_kernel(axis, me_ref, own, after, before, far0, far1, out_ref):
    shard = own.shape[1]

    def rows(offset):
        at = lax.rem(me_ref[axis] + offset, RING)
        return pl.ds(pl.multiple_of(at * shard, shard), shard)

    for offset, part in ((0, own), (1, after), (3, before)):
        out_ref[:, rows(offset)] = part[...]
    out_ref[0, rows(2)] = far0[...]
    out_ref[1, rows(2)] = far1[...]


def place(me, axis, parts):
    x, shard, half = parts[0].shape
    out = (shaped((x, RING * shard, half), BF16),)
    return call(functools.partial(place_kernel, axis), out, 0, (me,), *parts)[0]


def near_kernel(axis, offsets, me_ref, *refs):
    normeds, blocks = refs[:2], refs[2 : 2 + len(offsets)]
    begun, out_ref = refs[2 + len(offsets) : -1], refs[-1]
    depth = 2 * blocks[0].shape[1]
    for half, normed in enumerate(normeds):
        rows = slice(half * normed.shape[0], (half + 1) * normed.shape[0])
        total = begun[0][rows] if begun else None
        for offset, block in zip(offsets, blocks):
            at = pl.multiple_of(lax.rem(me_ref[axis] + offset, RING) * depth, depth)
            part = dot(normed[:, pl.ds(at, depth)], block[...].reshape(depth, -1))
            total = part if total is None else total + part
        out_ref[rows] = total


def project_near(me, axis, normeds, offsets, blocks, *begun):
    rows = 2 * normeds[0].shape[0]
    _, depth, cols = blocks[0].shape
    kernel = functools.partial(near_kernel, axis, offsets)
    out = (shaped((rows, cols), F32),)
    return call(kernel, out, 1.6 * len(blocks) * PEAK, (me,), *normeds, *blocks, *begun)[0]


def head_mean(values, spread, exact):
    wide = spread.shape[0]
    out = []
    for at in range(0, values.shape[-1], wide):
        part = values[:, at : at + wide]
        high = part.astype(BF16)
        mean = dot(high, spread)
        if not exact:
            mean = mean + dot((part - high.astype(F32)).astype(BF16), spread)
        out.append(mean)
    return jnp.concatenate(out, axis=-1)


def grad_block(turneds, x, at, axis, dproj):
    total = None
    for half, turned in enumerate(turneds):
        if axis == Y:
            part = turned[pl.ds(x * RING + at, 1)]
        else:
            part = turned[pl.ds(x * RING, RING), pl.ds(at, 1)]
        count = turned.shape[3]
        part = dot(part.reshape(RING * turned.shape[2], count), dproj[half * count : (half + 1) * count])
        total = part if total is None else total + part
    return total.astype(BF16)


def head_spread():
    of_row = lax.broadcasted_iota(jnp.int32, (4 * HEAD, 4 * HEAD), 0) // HEAD
    of_col = lax.broadcasted_iota(jnp.int32, (4 * HEAD, 4 * HEAD), 1) // HEAD
    return jnp.where(of_row == of_col, 1.0 / HEAD, 0.0).astype(BF16)


def centre_kernel(cot, out_ref):
    spread = head_spread()
    block = 256
    for at in range(0, cot.shape[0], block):
        part = cot[at : at + block]
        out_ref[at : at + block] = part.astype(F32) - head_mean(part, spread, True)


def centre(cot):
    return call(centre_kernel, (shaped(cot.shape, F32),), 0, (), cot)[0]


def far_kernel(axis, me_ref, cot, turned0, turned1, near, normed0, normed1, far0, far1, dproj_ref, *grad_refs):
    rows, cols = near.shape
    depth = 2 * far0.shape[0]
    block = 256
    spread = head_spread()
    far = lax.rem(me_ref[axis] + 2, RING)
    features = pl.ds(pl.multiple_of(far * depth, depth), depth)
    weight = jnp.concatenate([far0[...], far1[...]], axis=0)
    from_col = 0 if axis == Y else cols
    for at in range(0, rows, block):
        part = slice(at, at + block)
        normed, start = (normed0, normed1)[at // (rows // 2)], at % (rows // 2)
        proj = near[part] + dot(normed[start : start + block, features], weight)
        centred = proj - head_mean(proj, spread, False)
        scale = lax.rsqrt(head_mean(centred * centred, spread, True) + 1e-06)
        query = centred * scale
        cval = cot[part, from_col : from_col + cols]
        along = head_mean(cval * query, spread, False)
        dproj_ref[part] = (scale * (cval - query * along)).astype(BF16)
    for x in range(2):
        grad_refs[x][...] = grad_block((turned0, turned1), x, far, axis, dproj_ref)


def project_far(me, axis, cot, turneds, near, normeds, far0, far1):
    rows, cols = near.shape
    depth = far0.shape[0]
    out = (shaped((rows, cols), BF16),) + (shaped((depth, cols), BF16),) * 2
    kernel = functools.partial(far_kernel, axis)
    return call(kernel, out, 6 * PEAK, (me,), cot, *turneds, near, *normeds, far0, far1)


def rows_kernel(axis, offsets, me_ref, turned0, turned1, dproj, *outs):
    for offset, out_ref in zip(offsets, outs):
        at = lax.rem(me_ref[axis] + offset, RING)
        for x in range(2):
            out_ref[x] = grad_block((turned0, turned1), x, at, axis, dproj)


def grad_rows(me, axis, offsets, turneds, dproj):
    rows, cols = dproj.shape
    depth = RING * turneds[0].shape[2]
    out = (shaped((2, depth, cols), BF16),) * len(offsets)
    return call(functools.partial(rows_kernel, axis, offsets), out, 1.6 * len(out) * PEAK, (me,), *turneds, dproj)


def split_kernel(axis, me_ref, *refs):
    parts, outs = refs[:-RING], refs[-RING:]
    shard = outs[0].shape[1]
    for offset, out_ref in enumerate(outs):
        at = lax.rem(me_ref[axis] + offset, RING)
        rows = pl.ds(pl.multiple_of(at * shard, shard), shard)
        out_ref[...] = sum(part[:, rows].astype(F32) for part in parts).astype(BF16)


def split_sum(me, axis, parts):
    _, depth, cols = parts[0].shape
    out = (shaped((2, depth // RING, cols), BF16),) * RING
    return call(functools.partial(split_kernel, axis), out, 0, (me,), *parts)


def join_kernel(me_ref, *refs):
    kept_ref, sent_ref, away_ref = refs[2 * RING :]
    cols = refs[0].shape[-1]
    for half in range(2):
        parts = refs[RING * half : RING * (half + 1)]
        lanes = slice(half * cols, (half + 1) * cols)
        for outs, at in (((kept_ref, sent_ref), me_ref[X]), ((away_ref,), 1 - me_ref[X])):
            total = sum(part[pl.ds(at, 1)].astype(F32) for part in parts)[0]
            for out_ref in outs:
                out_ref[:, lanes] = total.astype(out_ref.dtype)


def join(me, parts):
    _, shard, cols = parts[0].shape
    out = (shaped((shard, 2 * cols), F32),) + (shaped((shard, 2 * cols), BF16),) * 2
    return call(join_kernel, out, 0, (me,), *parts)


def exchange(steps, sent, away):
    return (
        shift(away, ("rep", "xh"), (-steps, 1)),
        shift(away, "xh", 1),
        shift(sent, "rep", -steps),
    )


def add(a, b):
    return (a.astype(F32) + b.astype(F32)).astype(BF16)


def base_kernel(me_ref, weight, momentum, next1, next2, w_ref, m_ref):
    nearby = me_ref[APART] == 1
    w_ref[...] = 0.5 * (weight[...] + jnp.where(nearby, next1[0], next2[0]).astype(F32))
    m_ref[...] = 0.45 * (momentum[...] + jnp.where(nearby, next1[1], next2[1]).astype(F32))


def update_kernel(scale, rate_ref, base_w, base_m, own, got0, got1, got2, w_ref, m_ref):
    others = got0[...].astype(F32) + got1[...].astype(F32) + got2[...].astype(F32)
    out_m = base_m[...] + scale * (own[...] + others)
    m_ref[...] = out_m
    w_ref[...] = base_w[...] - rate_ref[0] * out_m


def on_device(tokens, cotangent, weight, momentum, step):
    local_w = weight[0]
    local_m = momentum[0]
    shard, width = local_w.shape
    apart = 1 + step % 2
    me = jnp.stack([lax.axis_index("xh"), lax.axis_index("y"), lax.axis_index("z"), apart]).astype(jnp.int32)
    rate = (jnp.float32(5e-05) * (step + 1).astype(F32))[None]
    wbf = local_w.astype(BF16)
    wbf, me, rate, apart = lax.optimization_barrier((wbf, me, rate, apart))
    pair = (shaped(local_w.shape, F32),) * 2

    wfar, norm0 = lax.optimization_barrier((shift(wbf, "xh", 1), norm_half(tokens[0], shard, 0)))
    half_a, half_b = order_x(me, wbf, wfar)
    parts_a, parts_b = (
        [part, shift(part, axis, -1), shift(part, axis, 1)] for part, axis in ((half_a, "z"), (half_b, "y"))
    )
    for parts, axis in ((parts_a, "z"), (parts_b, "y")):
        parts += [shift(parts[2][0], axis, 1), shift(parts[1][1], axis, -1)]
    parts_a, parts_b, norm0 = lax.optimization_barrier((parts_a, parts_b, norm0))
    own_a, own_b = place(me, Z, parts_a), place(me, Y, parts_b)
    tokens, _ = lax.optimization_barrier((tokens, own_b))
    ymajor, zmajor, turned = zip(norm0, norm_half(tokens[0], shard, 1))
    turned = [part.reshape(2 * RING, RING, shard, -1) for part in turned]
    cot = centre(cotangent[0])
    rings = (("y", Y, ymajor, own_a), ("z", Z, zmajor, own_b))
    around = []
    for axis, at, normed, block in rings:
        passed = [shift(block, axis, steps) for steps in (-1, 1)]
        around.append(
            lax.optimization_barrier((passed, project_near(me, at, normed, (0,), (block,)), turned, cot))
        )
    turned, cot = around[1][2:]
    far = [
        (shift(before[0], ring[0], 1), shift(after[1], ring[0], -1))
        for ring, ((after, before), *_) in zip(rings, around)
    ]
    begun = [
        project_near(me, at, normed, (1, 3), blocks, done)
        for (_, at, normed, _), (blocks, done, *_) in zip(rings, around)
    ]
    begun, turned = lax.optimization_barrier((begun, turned))
    dproj_a, far0_a, far1_a = project_far(me, Y, cot, turned, begun[0], ymajor, *far[0])
    up_a, down_a = shift(far0_a, "y", 1), shift(far1_a, "y", -1)
    dproj_a, begun_b = lax.optimization_barrier((dproj_a, begun[1]))
    dproj_b, far0_b, far1_b = project_far(me, Z, cot, turned, begun_b, zmajor, *far[1])
    up_b, down_b = shift(far0_b, "z", 1), shift(far1_b, "z", -1)
    dproj_a, dproj_b = lax.optimization_barrier((dproj_a, dproj_b))
    right_a, left_a = grad_rows(me, Y, (1, 3), turned, dproj_a)
    right_a = right_a.at[0].set(add(right_a[0], up_a))
    left_a = left_a.at[1].set(add(left_a[1], down_a))
    right_a, left_a, dproj_b = lax.optimization_barrier((right_a, left_a, dproj_b))
    right_a, left_a = shift(right_a, "y", 1), shift(left_a, "y", -1)
    right_b, left_b = grad_rows(me, Z, (1, 3), turned, dproj_b)
    right_b = right_b.at[0].set(add(right_b[0], up_b))
    left_b = left_b.at[1].set(add(left_b[1], down_b))
    right_b, left_b, dproj_a, dproj_b = lax.optimization_barrier((right_b, left_b, dproj_a, dproj_b))
    right_b, left_b = shift(right_b, "z", 1), shift(left_b, "z", -1)
    (own_a,) = grad_rows(me, Y, (0,), turned, dproj_a)
    (own_b,) = grad_rows(me, Z, (0,), turned, dproj_b)
    mine, own_a = lax.optimization_barrier((jnp.stack([local_w, local_m]), own_a))
    mine = mine.astype(BF16)
    base = call(base_kernel, pair, 0, (me,), local_w, local_m, shift(mine, "rep", -1), shift(mine, "rep", -2))
    own_b, base = lax.optimization_barrier((own_b, base))
    c = split_sum(me, Z, (own_a, right_a, left_a))
    sums = [c[0], shift(c[1], "z", 1), shift(c[3], "z", -1), shift(c[2], "z", 2)]
    c = split_sum(me, Y, (own_b, right_b, left_b))
    sums += [c[0], shift(c[1], "y", 1), shift(c[3], "y", -1), shift(c[2], "y", 2)]
    kept, sent, away, apart = lax.optimization_barrier((*join(me, sums), apart))
    got = lax.cond(apart == 1, functools.partial(exchange, 1), functools.partial(exchange, 2), sent, away)
    scale = 0.5 / (tokens.shape[1] * 2 * RING * RING) ** 0.5
    out_w, out_m = call(functools.partial(update_kernel, scale), pair, 0, (rate,), *base, kept, *got)
    return (out_w[None], out_m[None])


def solution(mesh):
    fine = Mesh(mesh.devices.reshape(mesh.shape["rep"], 2, RING, RING), ("rep", "xh", "y", "z"))
    rows = P("rep", ("xh", "y", "z"), None)
    return jax.shard_map(
        on_device,
        mesh=fine,
        in_specs=(rows, rows, rows, rows, P()),
        out_specs=(rows, rows),
        check_vma=False,
    )
```

```python
import functools

import jax
import jax.numpy as jnp
from jax import lax
from jax.experimental import pallas as pl
from jax.experimental.pallas import tpu as pltpu
from jax.sharding import Mesh, PartitionSpec as P

HEAD = 64
F32 = jnp.float32
BF16 = jnp.bfloat16
RING = 4
X, Y, Z, APART = range(4)
PEAK = 1.1e9
VMEM = pl.BlockSpec(memory_space=pltpu.VMEM)
SMEM = pl.BlockSpec(memory_space=pltpu.SMEM)


def shift(value, axis, steps):
    axes, steps = ((axis,), (steps,)) if isinstance(axis, str) else (axis, steps)
    sizes = [lax.axis_size(name) for name in axes]
    pairs = [(0, 0)]
    for size, step in zip(sizes, steps):
        pairs = [(s * size + i, t * size + (i + step) % size) for s, t in pairs for i in range(size)]
    return lax.ppermute(value, axes if len(axes) > 1 else axes[0], pairs)


def shaped(shape, dtype):
    return jax.ShapeDtypeStruct(shape, dtype)


def call(kernel, out_shape, flops, scalars, *arrays, aliases={}):
    return pl.pallas_call(
        kernel,
        out_shape=out_shape,
        in_specs=[SMEM] * len(scalars) + [VMEM] * len(arrays),
        out_specs=tuple(VMEM for _ in out_shape),
        input_output_aliases=aliases,
        compiler_params=pltpu.CompilerParams(vmem_limit_bytes=10 * 1024 * 1024),
        cost_estimate=pl.CostEstimate(flops=int(flops), bytes_accessed=0, transcendentals=0),
    )(*scalars, *arrays)


def dot(a, b):
    return jnp.dot(a, b, preferred_element_type=F32)


def norm_kernel(shard, start, tok_ref, *refs):
    ymajor_ref, zmajor_ref, turned_ref = refs[-3:]
    block = 128
    order_y = [(x * RING + y) * RING * shard for y in range(RING) for x in range(2)]
    order_z = [((x * RING + y) * RING + z) * shard for z in range(RING) for x in range(2) for y in range(RING)]

    @pl.loop(0, ymajor_ref.shape[0] // block)
    def _(i):
        at = pl.ds(pl.multiple_of(i * block, block), block)
        xf = tok_ref[pl.ds(pl.multiple_of(start + i * block, block), block)].astype(F32)
        mean = jnp.mean(xf, axis=-1, keepdims=True)
        centred = xf - mean
        var = jnp.mean(centred * centred, axis=-1, keepdims=True)
        normed = centred * lax.rsqrt(var + 1e-05)
        small = normed.astype(BF16)
        run = RING * shard
        ymajor_ref[at] = jnp.concatenate([small[:, k : k + run] for k in order_y], axis=-1)
        zmajor_ref[at] = jnp.concatenate([normed[:, k : k + shard] for k in order_z], axis=-1).astype(BF16)
        turned_ref[:, pl.ds(pl.multiple_of(start + i * block, block), block)] = small.T


def norm_half(tokens, shard, half, *turned):
    rows, width = tokens.shape[0] // 2, tokens.shape[1]
    out = (shaped((rows, width), BF16), shaped((rows, width), BF16), shaped((width, 2 * rows), BF16))
    kernel = functools.partial(norm_kernel, shard, half * rows)
    return call(kernel, out, 8 * rows * width, (), tokens, *turned, aliases={1: 2} if turned else {})


def order_kernel(me_ref, mine, other, a_ref, b_ref):
    half = a_ref.shape[-1]
    for part, at in ((mine, me_ref[X]), (other, 1 - me_ref[X])):
        a_ref[pl.ds(at, 1)] = part[:, :half][None]
        b_ref[pl.ds(at, 1)] = part[:, half:][None]


def order_x(me, mine, other):
    shard, width = mine.shape
    out = (shaped((2, shard, width // 2), BF16),) * 2
    return call(order_kernel, out, 0, (me,), mine, other)


def place_kernel(axis, me_ref, own, after, before, far0, far1, out_ref):
    shard = own.shape[1]

    def rows(offset):
        at = lax.rem(me_ref[axis] + offset, RING)
        return pl.ds(pl.multiple_of(at * shard, shard), shard)

    for offset, part in ((0, own), (1, after), (3, before)):
        out_ref[:, rows(offset)] = part[...]
    out_ref[0, rows(2)] = far0[...]
    out_ref[1, rows(2)] = far1[...]


def place(me, axis, parts):
    x, shard, half = parts[0].shape
    out = (shaped((x, RING * shard, half), BF16),)
    return call(functools.partial(place_kernel, axis), out, 0, (me,), *parts)[0]


def near_kernel(axis, offsets, me_ref, *refs):
    normeds, blocks = refs[:2], refs[2 : 2 + len(offsets)]
    begun, out_ref = refs[2 + len(offsets) : -1], refs[-1]
    depth = 2 * blocks[0].shape[1]
    for half, normed in enumerate(normeds):
        rows = slice(half * normed.shape[0], (half + 1) * normed.shape[0])
        total = begun[0][rows] if begun else None
        for offset, block in zip(offsets, blocks):
            at = pl.multiple_of(lax.rem(me_ref[axis] + offset, RING) * depth, depth)
            part = dot(normed[:, pl.ds(at, depth)], block[...].reshape(depth, -1))
            total = part if total is None else total + part
        out_ref[rows] = total


def project_near(me, axis, normeds, offsets, blocks, *begun):
    rows = 2 * normeds[0].shape[0]
    _, depth, cols = blocks[0].shape
    kernel = functools.partial(near_kernel, axis, offsets)
    out = (shaped((rows, cols), F32),)
    return call(kernel, out, 1.6 * len(blocks) * PEAK, (me,), *normeds, *blocks, *begun)[0]


def head_mean(values, spread, exact):
    wide = spread.shape[0]
    out = []
    for at in range(0, values.shape[-1], wide):
        part = values[:, at : at + wide]
        high = part.astype(BF16)
        mean = dot(high, spread)
        if not exact:
            mean = mean + dot((part - high.astype(F32)).astype(BF16), spread)
        out.append(mean)
    return jnp.concatenate(out, axis=-1)


def grad_block(turneds, x, at, axis, dproj):
    total = None
    for half, turned in enumerate(turneds):
        if axis == Y:
            part = turned[pl.ds(x * RING + at, 1)]
        else:
            part = turned[pl.ds(x * RING, RING), pl.ds(at, 1)]
        count = turned.shape[3]
        part = dot(part.reshape(RING * turned.shape[2], count), dproj[half * count : (half + 1) * count])
        total = part if total is None else total + part
    return total.astype(BF16)


def head_spread():
    of_row = lax.broadcasted_iota(jnp.int32, (4 * HEAD, 4 * HEAD), 0) // HEAD
    of_col = lax.broadcasted_iota(jnp.int32, (4 * HEAD, 4 * HEAD), 1) // HEAD
    return jnp.where(of_row == of_col, 1.0 / HEAD, 0.0).astype(BF16)


def centre_kernel(cot, out_ref):
    spread = head_spread()
    block = 256
    for at in range(0, cot.shape[0], block):
        part = cot[at : at + block]
        out_ref[at : at + block] = part.astype(F32) - head_mean(part, spread, True)


def centre(cot):
    return call(centre_kernel, (shaped(cot.shape, F32),), 0, (), cot)[0]


def far_kernel(axis, me_ref, cot, turned, near, normed0, normed1, far0, far1, dproj_ref, *grad_refs):
    rows, cols = near.shape
    depth = 2 * far0.shape[0]
    block = 256
    spread = head_spread()
    far = lax.rem(me_ref[axis] + 2, RING)
    features = pl.ds(pl.multiple_of(far * depth, depth), depth)
    weight = jnp.concatenate([far0[...], far1[...]], axis=0)
    from_col = 0 if axis == Y else cols
    for at in range(0, rows, block):
        part = slice(at, at + block)
        normed, start = (normed0, normed1)[at // (rows // 2)], at % (rows // 2)
        proj = near[part] + dot(normed[start : start + block, features], weight)
        centred = proj - head_mean(proj, spread, False)
        scale = lax.rsqrt(head_mean(centred * centred, spread, True) + 1e-06)
        query = centred * scale
        cval = cot[part, from_col : from_col + cols]
        along = head_mean(cval * query, spread, False)
        dproj_ref[part] = (scale * (cval - query * along)).astype(BF16)
    for x in range(2):
        grad_refs[x][...] = grad_block((turned,), x, far, axis, dproj_ref)


def project_far(me, axis, cot, turneds, near, normeds, far0, far1):
    rows, cols = near.shape
    depth = far0.shape[0]
    out = (shaped((rows, cols), BF16),) + (shaped((depth, cols), BF16),) * 2
    kernel = functools.partial(far_kernel, axis)
    return call(kernel, out, 6 * PEAK, (me,), cot, *turneds, near, *normeds, far0, far1)


def rows_kernel(axis, offsets, me_ref, turned, dproj, *outs):
    for offset, out_ref in zip(offsets, outs):
        at = lax.rem(me_ref[axis] + offset, RING)
        for x in range(2):
            out_ref[x] = grad_block((turned,), x, at, axis, dproj)


def grad_rows(me, axis, offsets, turneds, dproj):
    rows, cols = dproj.shape
    depth = RING * turneds[0].shape[2]
    out = (shaped((2, depth, cols), BF16),) * len(offsets)
    return call(functools.partial(rows_kernel, axis, offsets), out, 1.6 * len(out) * PEAK, (me,), *turneds, dproj)


def split_kernel(axis, me_ref, *refs):
    parts, outs = refs[:-RING], refs[-RING:]
    shard = outs[0].shape[1]
    for offset, out_ref in enumerate(outs):
        at = lax.rem(me_ref[axis] + offset, RING)
        rows = pl.ds(pl.multiple_of(at * shard, shard), shard)
        out_ref[...] = sum(part[:, rows].astype(F32) for part in parts).astype(BF16)


def split_sum(me, axis, parts):
    _, depth, cols = parts[0].shape
    out = (shaped((2, depth // RING, cols), BF16),) * RING
    return call(functools.partial(split_kernel, axis), out, 0, (me,), *parts)


def join_kernel(me_ref, *refs):
    kept_ref, sent_ref, away_ref = refs[2 * RING :]
    cols = refs[0].shape[-1]
    for half in range(2):
        parts = refs[RING * half : RING * (half + 1)]
        lanes = slice(half * cols, (half + 1) * cols)
        for outs, at in (((kept_ref, sent_ref), me_ref[X]), ((away_ref,), 1 - me_ref[X])):
            total = sum(part[pl.ds(at, 1)].astype(F32) for part in parts)[0]
            for out_ref in outs:
                out_ref[:, lanes] = total.astype(out_ref.dtype)


def join(me, parts):
    _, shard, cols = parts[0].shape
    out = (shaped((shard, 2 * cols), F32),) + (shaped((shard, 2 * cols), BF16),) * 2
    return call(join_kernel, out, 0, (me,), *parts)


def exchange(steps, sent, away):
    return (
        shift(away, ("rep", "xh"), (-steps, 1)),
        shift(away, "xh", 1),
        shift(sent, "rep", -steps),
    )


def add(a, b):
    return (a.astype(F32) + b.astype(F32)).astype(BF16)


def base_kernel(me_ref, weight, momentum, next1, next2, w_ref, m_ref):
    nearby = me_ref[APART] == 1
    w_ref[...] = 0.5 * (weight[...] + jnp.where(nearby, next1[0], next2[0]).astype(F32))
    m_ref[...] = 0.45 * (momentum[...] + jnp.where(nearby, next1[1], next2[1]).astype(F32))


def update_kernel(scale, rate_ref, base_w, base_m, own, got0, got1, got2, w_ref, m_ref):
    others = got0[...].astype(F32) + got1[...].astype(F32) + got2[...].astype(F32)
    out_m = base_m[...] + scale * (own[...] + others)
    m_ref[...] = out_m
    w_ref[...] = base_w[...] - rate_ref[0] * out_m


def on_device(tokens, cotangent, weight, momentum, step):
    local_w = weight[0]
    local_m = momentum[0]
    shard, width = local_w.shape
    apart = 1 + step % 2
    me = jnp.stack([lax.axis_index("xh"), lax.axis_index("y"), lax.axis_index("z"), apart]).astype(jnp.int32)
    rate = (jnp.float32(5e-05) * (step + 1).astype(F32))[None]
    wbf = local_w.astype(BF16)
    wbf, me, rate, apart = lax.optimization_barrier((wbf, me, rate, apart))
    pair = (shaped(local_w.shape, F32),) * 2

    wfar, norm0 = lax.optimization_barrier((shift(wbf, "xh", 1), norm_half(tokens[0], shard, 0)))
    half_a, half_b = order_x(me, wbf, wfar)
    parts_a, parts_b = (
        [part, shift(part, axis, -1), shift(part, axis, 1)] for part, axis in ((half_a, "z"), (half_b, "y"))
    )
    for parts, axis in ((parts_a, "z"), (parts_b, "y")):
        parts += [shift(parts[2][0], axis, 1), shift(parts[1][1], axis, -1)]
    parts_a, parts_b, norm0 = lax.optimization_barrier((parts_a, parts_b, norm0))
    own_a, own_b = place(me, Z, parts_a), place(me, Y, parts_b)
    tokens, _ = lax.optimization_barrier((tokens, own_b))
    norm1 = norm_half(tokens[0], shard, 1, norm0[2])
    ymajor, zmajor, turned = (norm0[0], norm1[0]), (norm0[1], norm1[1]), norm1[2:]
    turned = [part.reshape(2 * RING, RING, shard, -1) for part in turned]
    cot = centre(cotangent[0])
    rings = (("y", Y, ymajor, own_a), ("z", Z, zmajor, own_b))
    around = []
    for axis, at, normed, block in rings:
        passed = [shift(block, axis, steps) for steps in (-1, 1)]
        around.append(
            lax.optimization_barrier((passed, project_near(me, at, normed, (0,), (block,)), turned, cot))
        )
    turned, cot = around[1][2:]
    far = [
        (shift(before[0], ring[0], 1), shift(after[1], ring[0], -1))
        for ring, ((after, before), *_) in zip(rings, around)
    ]
    begun = [
        project_near(me, at, normed, (1, 3), blocks, done)
        for (_, at, normed, _), (blocks, done, *_) in zip(rings, around)
    ]
    begun, turned = lax.optimization_barrier((begun, turned))
    dproj_a, far0_a, far1_a = project_far(me, Y, cot, turned, begun[0], ymajor, *far[0])
    up_a, down_a = shift(far0_a, "y", 1), shift(far1_a, "y", -1)
    dproj_a, begun_b = lax.optimization_barrier((dproj_a, begun[1]))
    dproj_b, far0_b, far1_b = project_far(me, Z, cot, turned, begun_b, zmajor, *far[1])
    up_b, down_b = shift(far0_b, "z", 1), shift(far1_b, "z", -1)
    dproj_a, dproj_b = lax.optimization_barrier((dproj_a, dproj_b))
    right_a, left_a = grad_rows(me, Y, (1, 3), turned, dproj_a)
    right_a = right_a.at[0].set(add(right_a[0], up_a))
    left_a = left_a.at[1].set(add(left_a[1], down_a))
    right_a, left_a, dproj_b = lax.optimization_barrier((right_a, left_a, dproj_b))
    right_a, left_a = shift(right_a, "y", 1), shift(left_a, "y", -1)
    right_b, left_b = grad_rows(me, Z, (1, 3), turned, dproj_b)
    right_b = right_b.at[0].set(add(right_b[0], up_b))
    left_b = left_b.at[1].set(add(left_b[1], down_b))
    right_b, left_b, dproj_a, dproj_b = lax.optimization_barrier((right_b, left_b, dproj_a, dproj_b))
    right_b, left_b = shift(right_b, "z", 1), shift(left_b, "z", -1)
    (own_a,) = grad_rows(me, Y, (0,), turned, dproj_a)
    (own_b,) = grad_rows(me, Z, (0,), turned, dproj_b)
    mine, own_a = lax.optimization_barrier((jnp.stack([local_w, local_m]), own_a))
    mine = mine.astype(BF16)
    base = call(base_kernel, pair, 0, (me,), local_w, local_m, shift(mine, "rep", -1), shift(mine, "rep", -2))
    own_b, base = lax.optimization_barrier((own_b, base))
    c = split_sum(me, Z, (own_a, right_a, left_a))
    sums = [c[0], shift(c[1], "z", 1), shift(c[3], "z", -1), shift(c[2], "z", 2)]
    c = split_sum(me, Y, (own_b, right_b, left_b))
    sums += [c[0], shift(c[1], "y", 1), shift(c[3], "y", -1), shift(c[2], "y", 2)]
    kept, sent, away, apart = lax.optimization_barrier((*join(me, sums), apart))
    got = lax.cond(apart == 1, functools.partial(exchange, 1), functools.partial(exchange, 2), sent, away)
    scale = 0.5 / (tokens.shape[1] * 2 * RING * RING) ** 0.5
    out_w, out_m = call(functools.partial(update_kernel, scale), pair, 0, (rate,), *base, kept, *got)
    return (out_w[None], out_m[None])


def solution(mesh):
    fine = Mesh(mesh.devices.reshape(mesh.shape["rep"], 2, RING, RING), ("rep", "xh", "y", "z"))
    rows = P("rep", ("xh", "y", "z"), None)
    return jax.shard_map(
        on_device,
        mesh=fine,
        in_specs=(rows, rows, rows, rows, P()),
        out_specs=(rows, rows),
        check_vma=False,
    )
```
